32 devices in a mesh: groups: 2 (over x), ctx: 16 (over z, y, core).
Axes of the slice: x: 2, y: 2, z: 4, core: 2. Of those that a mesh axis runs over, the one named last changes fastest.
Arguments:
- queries: bfloat16 [4096, 1024], P(('groups', 'ctx')), parts along dimension 0, may hold values from -128 to 128
- keys: bfloat16 [4096, 256], P(('groups', 'ctx')), parts along dimension 0, may hold values from -32 to 32
- values: bfloat16 [4096, 256], P(('groups', 'ctx')), parts along dimension 0, may hold values from -6 to 6
- lengths: int32 [16], P('groups'), parts along dimension 0, may hold values from 1 to 1024, 2048 in all
- d_out: bfloat16 [4096, 1024], P(('groups', 'ctx')), parts along dimension 0, may hold values from -6 to 6
Outputs:
- attended: bfloat16 [4096, 1024], P(('groups', 'ctx')), parts along dimension 0
- grad_q: bfloat16 [4096, 1024], P(('groups', 'ctx')), parts along dimension 0
- grad_k: bfloat16 [4096, 256], P(('groups', 'ctx')), parts along dimension 0
- grad_v: bfloat16 [4096, 256], P(('groups', 'ctx')), parts along dimension 0
The draws below stay inside these ranges and needn't reach their ends.
There are 2 independent parts, one for each index of `groups`. The reference program is written for one: setup_inputs(seed, part) draws one part's arguments, and reference() takes and returns one part's arrays. A program takes and returns all parts, laid end to end along the dimension named above; each array names one. Nothing has to cross between parts.
All inputs are finite; a program needn't handle non-finite values.
Results may differ from the reference program's by a relative error of at most 0.012.
The reference program's roundings to bfloat16 on the way (of `weights` and `dscores`) count: a program that leaves them out, or rounds other values in their place, can miss the bound.
Values may be sent and summed in bfloat16 or wider, within the bound.
A program may use at most 64 MiB of HBM per device.

```python
import math
import jax
import jax.numpy as jnp
import numpy as np
from jax import lax

HEADS = 8
KV_HEADS = 2
HEAD_DIM = 128
KV_BLOCKS = 8
TOK_DEV = 128
TOKENS = 2048
DOC_MAX = 1024
DOCS = 8
N_CTX = 16


def draw_keys(key, part):
    key = jax.random.fold_in(key, 1)
    full_shape = (TOKENS, KV_HEADS * HEAD_DIM)
    result = jnp.clip(jax.random.normal(key, full_shape, jnp.float32), -6.0, 6.0)
    return result.astype(jnp.bfloat16)


def draw_queries(key, part):
    key = jax.random.fold_in(key, 2)
    full_shape = (TOKENS, HEADS * HEAD_DIM)
    result = jnp.clip(jax.random.normal(key, full_shape, jnp.float32), -6.0, 6.0)
    return result.astype(jnp.bfloat16)


def block_scale(own_key, extent, split, smallest, high):
    def one(dim, parts):
        steps = jax.random.uniform(jax.random.fold_in(jax.random.fold_in(own_key, 6), dim), (parts,), jnp.float32, smallest / len(split), high / len(split))
        return jnp.repeat(jnp.exp(steps), extent[dim] // parts).reshape((-1,) + (1,) * (len(extent) - dim - 1))

    loudness = one(*split[0])
    for cut in split[1:]:
        loudness = loudness * one(*cut)
    return loudness


def profile(number_of, total, limit, slope):
    weights = [(1 << 20) // math.isqrt(standing ** slope) + 1 for standing in range(2, number_of + 1)]
    rest, holding = total - limit - (number_of - 1), [1] * (number_of - 1)
    while rest > 0:
        candidates = [i for i in range(number_of - 1) if holding[i] < limit]
        whole, remaining = sum([weights[i] for i in candidates]), rest
        for i in candidates:
            more = min(limit - holding[i], max(1, remaining * weights[i] // whole), rest)
            holding[i] = holding[i] + more
            rest = rest - more
    return np.array([limit] + holding)


def ragged(stream_key, amount, total, bound, skew):
    if amount == 2:
        one = jax.random.randint(stream_key, (), max(1, total - bound), min(bound, total - 1) + 1)
        return jnp.stack([one, total - one])
    sizes = jnp.asarray(profile(amount, total, bound, skew), jnp.int32)
    pairs = (amount - 1) // 2
    giver, taker = sizes[1:1 + 2 * pairs:2], sizes[2:2 + 2 * pairs:2]
    margin = jnp.minimum(giver - 1, bound - taker)
    passed = jax.random.randint(jax.random.fold_in(stream_key, 1), (pairs,), 0, 1 << 20) % (margin + 1)
    sizes = sizes.at[1:1 + 2 * pairs:2].set(giver - passed).at[2:2 + 2 * pairs:2].set(taker + passed)
    return sizes[jax.random.permutation(jax.random.fold_in(stream_key, 2), amount)]


def bell_draw(stream_key, dims, spread, bound, shards=(), held_as=jnp.bfloat16):
    values = jax.random.normal(stream_key, dims, jnp.float32) * spread
    if len(shards) > 0:
        values = block_scale(stream_key, dims, shards, -0.22, 0.18) * values
    return jnp.clip(values, min=-bound, max=bound).astype(held_as)


def setup_inputs(seed: int = 0, part: int = 0) -> dict:
    key_list = jax.random.split(jax.random.key(seed), 6)
    part_splits = jax.random.split(jax.random.fold_in(key_list[5], part), 6)
    queries = draw_queries(jax.random.fold_in(jax.random.fold_in(key_list[5], part), 71), part)
    keys = draw_keys(jax.random.fold_in(jax.random.fold_in(key_list[5], part), 71), part)
    values = bell_draw(part_splits[2], (TOKENS, KV_HEADS * HEAD_DIM), 1.0, 6.0, ((0, 16),))
    lengths = ragged(part_splits[3], DOCS, TOKENS, DOC_MAX, 2).astype(jnp.int32)
    d_out = bell_draw(part_splits[4], (TOKENS, HEADS * HEAD_DIM), 1.0, 6.0, ((0, 16),))
    return dict(queries=queries, keys=keys, values=values, lengths=lengths, d_out=d_out)


MASKED_SCORE = -1e30


def doc_index(positions, doc_ends):
    return jnp.sum((positions[:, None] >= doc_ends[None, :]).astype(jnp.int32), axis=1)


def score_block(query_heads, key_block, allowed):
    key_heads = key_block.astype(jnp.float32).reshape(key_block.shape[0], KV_HEADS, HEAD_DIM)
    scores = jnp.einsum("qgrd,kgd->grqk", query_heads.astype(jnp.float32), key_heads)
    return jnp.where(allowed, scores * (HEAD_DIM ** -0.5), MASKED_SCORE)


def running_stats(stats_pair, scores):
    row_max, row_sum = stats_pair
    new_max = jnp.maximum(row_max, jnp.max(scores, axis=-1))
    row_sum = row_sum * jnp.exp(row_max - new_max) + jnp.sum(jnp.exp(scores - new_max[..., None]), axis=-1)
    return new_max, row_sum


def output_term(query_heads, kv_block, allowed, log_norm):
    scores = score_block(query_heads, kv_block[0], allowed)
    weights = jnp.exp(scores - log_norm[..., None]).astype(jnp.bfloat16)
    value_heads = kv_block[1].astype(jnp.float32).reshape(kv_block.shape[1], KV_HEADS, HEAD_DIM)
    return jnp.einsum("grqk,kgd->qgrd", weights.astype(jnp.float32), value_heads)


def gradient_term(query_heads, grad_heads, kv_block, allowed, log_norm, delta_rows):
    rows_here = kv_block.shape[1]
    key_heads = kv_block[0].astype(jnp.float32).reshape(rows_here, KV_HEADS, HEAD_DIM)
    value_heads = kv_block[1].astype(jnp.float32).reshape(rows_here, KV_HEADS, HEAD_DIM)
    scores = score_block(query_heads, kv_block[0], allowed)
    exp_weights = jnp.exp(scores - log_norm[..., None])
    weights = exp_weights.astype(jnp.bfloat16).astype(jnp.float32)
    grad_float = grad_heads.astype(jnp.float32)
    dv_term = jnp.einsum("grqk,qgrd->kgd", weights, grad_float)
    dprobs = jnp.einsum("qgrd,kgd->grqk", grad_float, value_heads)
    dscores = (exp_weights * (dprobs - delta_rows[..., None])).astype(jnp.bfloat16).astype(jnp.float32)
    dq_term = jnp.einsum("grqk,kgd->qgrd", dscores, key_heads)
    dk_term = jnp.einsum("grqk,qgrd->kgd", dscores, query_heads.astype(jnp.float32))
    return dq_term, jnp.stack([dk_term.reshape(rows_here, -1), dv_term.reshape(rows_here, -1)])


def reference(queries, keys, values, lengths, d_out):
    per_group = HEADS // KV_HEADS
    kv_width = KV_HEADS * HEAD_DIM
    doc_ends = jnp.cumsum(lengths).astype(jnp.int32)
    zero_front = jnp.zeros((KV_BLOCKS * TOK_DEV, kv_width), keys.dtype)
    key_pad = jnp.concatenate([zero_front, keys], axis=0)
    value_pad = jnp.concatenate([zero_front, values], axis=0)
    offsets = jnp.arange(TOK_DEV, dtype=jnp.int32)
    padded_rows = (N_CTX + KV_BLOCKS) * TOK_DEV

    def block_step(accum, block_index):
        q_pos = block_index * TOK_DEV + offsets
        q_doc = doc_index(q_pos, doc_ends)
        q_block = lax.dynamic_slice_in_dim(queries, block_index * TOK_DEV, TOK_DEV, 0)
        g_block = lax.dynamic_slice_in_dim(d_out, block_index * TOK_DEV, TOK_DEV, 0)
        query_heads = q_block.reshape(TOK_DEV, KV_HEADS, per_group, HEAD_DIM)
        grad_heads = g_block.reshape(TOK_DEV, KV_HEADS, per_group, HEAD_DIM)
        blocks = []
        for distance in range(KV_BLOCKS + 1):
            start = ((block_index - distance + KV_BLOCKS) * TOK_DEV).astype(jnp.int32)
            kv_block = jnp.stack([lax.dynamic_slice_in_dim(key_pad, start, TOK_DEV, 0), lax.dynamic_slice_in_dim(value_pad, start, TOK_DEV, 0)])
            k_pos = (block_index - distance) * TOK_DEV + offsets
            k_doc = doc_index(k_pos, doc_ends)
            allowed = (q_doc[:, None] == k_doc[None, :]) & (k_pos[None, :] <= q_pos[:, None]) & (k_pos[None, :] >= 0)
            is_live = (q_doc[0] == k_doc[TOK_DEV - 1]) & (block_index >= distance)
            blocks.append((kv_block, allowed, is_live, start))

        stats_pair = (jnp.full((KV_HEADS, per_group, TOK_DEV), MASKED_SCORE, jnp.float32), jnp.zeros((KV_HEADS, per_group, TOK_DEV), jnp.float32))
        for distance in range(KV_BLOCKS + 1):
            kv_block, allowed, is_live, start = blocks[distance]

            def stats_live(stats_in, kv_here, allow_here):
                return running_stats(stats_in, score_block(query_heads, kv_here[0], allow_here))

            def stats_dead(stats_in, kv_here, allow_here):
                return stats_in

            if distance == 0:
                stats_pair = stats_live(stats_pair, kv_block, allowed)
            else:
                stats_pair = lax.cond(is_live, stats_live, stats_dead, stats_pair, kv_block, allowed)
        log_norm = stats_pair[0] + jnp.log(stats_pair[1])

        summed = jnp.zeros((TOK_DEV, KV_HEADS, per_group, HEAD_DIM), jnp.float32)
        for distance in range(KV_BLOCKS + 1):
            kv_block, allowed, is_live, start = blocks[distance]

            def out_live(kv_here, allow_here):
                return output_term(query_heads, kv_here, allow_here, log_norm)

            def out_dead(kv_here, allow_here):
                return jnp.zeros((TOK_DEV, KV_HEADS, per_group, HEAD_DIM), jnp.float32)

            if distance == 0:
                summed = summed + out_live(kv_block, allowed)
            else:
                summed = summed + lax.cond(is_live, out_live, out_dead, kv_block, allowed)
        attended_block = summed.reshape(TOK_DEV, HEADS * HEAD_DIM).astype(jnp.bfloat16)
        delta_rows = jnp.sum((attended_block.astype(jnp.float32) * g_block.astype(jnp.float32)).reshape(TOK_DEV, KV_HEADS, per_group, HEAD_DIM), axis=-1).transpose(1, 2, 0)

        dq_summed = jnp.zeros((TOK_DEV, KV_HEADS, per_group, HEAD_DIM), jnp.float32)
        grad_acc = accum
        for distance in range(KV_BLOCKS + 1):
            kv_block, allowed, is_live, start = blocks[distance]

            def grad_live(kv_here, allow_here):
                return gradient_term(query_heads, grad_heads, kv_here, allow_here, log_norm, delta_rows)

            def grad_dead(kv_here, allow_here):
                return (jnp.zeros((TOK_DEV, KV_HEADS, per_group, HEAD_DIM), jnp.float32), jnp.zeros((2, TOK_DEV, kv_width), jnp.float32))

            if distance == 0:
                dq_term, kv_part = grad_live(kv_block, allowed)
            else:
                dq_term, kv_part = lax.cond(is_live, grad_live, grad_dead, kv_block, allowed)
            dq_summed = dq_summed + dq_term
            grad_acc = lax.dynamic_update_slice_in_dim(grad_acc, lax.dynamic_slice_in_dim(grad_acc, start, TOK_DEV, 1) + kv_part, start, 1)
        grad_q_block = (dq_summed * (HEAD_DIM ** -0.5)).reshape(TOK_DEV, HEADS * HEAD_DIM).astype(jnp.bfloat16)
        return grad_acc, (attended_block, grad_q_block)

    initial = jnp.zeros((2, padded_rows, kv_width), jnp.float32)
    grad_acc, (attended_all, grad_q_all) = lax.scan(block_step, initial, jnp.arange(N_CTX, dtype=jnp.int32))
    attended = attended_all.reshape(TOKENS, HEADS * HEAD_DIM)
    grad_q = grad_q_all.reshape(TOKENS, HEADS * HEAD_DIM)
    grad_k = (grad_acc[0, KV_BLOCKS * TOK_DEV:] * (HEAD_DIM ** -0.5)).astype(jnp.bfloat16)
    grad_v = grad_acc[1, KV_BLOCKS * TOK_DEV:].astype(jnp.bfloat16)
    return (attended, grad_q, grad_k, grad_v)
```

```python
import functools

import jax
import jax.numpy as jnp
from jax import lax
from jax.experimental import pallas as pl
from jax.experimental.pallas import tpu as pltpu
from jax.sharding import PartitionSpec as P

HEADS = 8
KV_HEADS = 2
HEAD_DIM = 128
KV_BLOCKS = 8
PER_GROUP = HEADS // KV_HEADS
SLOTS = KV_BLOCKS // 2 + 1
MASKED_SCORE = -1e30
SCALE = HEAD_DIM ** (-0.5)
MESH = pl.DeviceIdType.MESH
F32 = jnp.float32
BF16 = jnp.bfloat16


def dot_nt(a, b):
    return lax.dot_general(a, b, (((1,), (1,)), ((), ())), preferred_element_type=F32)


def dot_nn(a, b):
    return lax.dot_general(a, b, (((1,), (0,)), ((), ())), preferred_element_type=F32)


def kernel(
    chips, len_ref, q_in, k_in, v_in, g_in,
    att_out, dq_out, dk_out, dv_out,
    k_buf, v_buf, q_buf, g_buf, qt, gt, bias, e_scr, dp_scr, w_scr, ds_scr,
    m_scr, l_scr, f_scr, part, y_got, z_got, att_s, dq_s, dk_s, dv_s,
    in_local, in_send, in_recv, kv_recv, kv_zs, kv_ys,
    gy_send, gy_recv, gz_send, gz_recv, out_local, out_send, out_recv,
):
    tok = q_in.shape[0]
    rows = 2 * tok
    width = PER_GROUP * HEAD_DIM
    me = lax.axis_index("ctx")
    core = lax.rem(me, 2)
    chip = lax.div(me, 2)
    odd = lax.rem(chip, 2) == 1
    even = lax.rem(chip, 2) == 0
    sib = me + 1 - 2 * core
    side = me + 2 - 4 * lax.rem(chip, 2)
    up = me + 4
    down = me - 4
    has_up = chip + 2 < chips
    has_down = chip >= 2

    def remote(src, dst, ssem, rsem, dev):
        return pltpu.make_async_remote_copy(
            src_ref=src, dst_ref=dst, send_sem=ssem, recv_sem=rsem,
            device_id={"ctx": dev}, device_id_type=MESH,
        )

    def own_rows(c):
        return pl.ds(pl.multiple_of(c * tok, tok), tok)

    def cols(c, size):
        return pl.ds(pl.multiple_of(c * size, size), size)

    def slot(j):
        return pl.ds(j * rows, rows)

    ins = ((k_in, k_buf, HEAD_DIM), (v_in, v_buf, HEAD_DIM), (q_in, q_buf, width), (g_in, g_buf, width))
    loads = []
    trades = []
    for i, (src, dst, size) in enumerate(ins):
        loads.append(pltpu.make_async_copy(
            src.at[:, cols(core, size)], dst.at[own_rows(core), :], in_local.at[i]))
        trades.append(remote(
            src.at[:, cols(1 - core, size)], dst.at[own_rows(core), :],
            in_send.at[i], in_recv.at[i], sib))
    for load in loads:
        load.start()

    barrier = pltpu.get_barrier_semaphore()

    def greet(dev):
        pl.semaphore_signal(barrier, inc=1, device_id={"ctx": dev}, device_id_type=MESH)

    greet(sib)
    greet(side)

    @pl.when(has_up)
    def _():
        greet(up)

    @pl.when(has_down)
    def _():
        greet(down)

    peers = 2 + has_up.astype(jnp.int32) + has_down.astype(jnp.int32)
    pl.semaphore_wait(barrier, peers)

    for trade in trades:
        trade.start()

    bufs = (k_buf, v_buf)

    def kv_z(msg, t):
        return remote(bufs[t].at[slot(2 * msg)], bufs[t].at[slot(2 * msg + 2)],
                      kv_zs.at[msg, t], kv_recv.at[2 * msg + 2, t], up)

    def kv_y(msg, t, src):
        return remote(bufs[t].at[slot(src)], bufs[t].at[slot(2 * msg + 1)],
                      kv_ys.at[msg, t], kv_recv.at[2 * msg + 1, t], side)

    def kv_arrived(j, t):
        remote(bufs[t].at[slot(j)], bufs[t].at[slot(j)],
               kv_zs.at[0, t], kv_recv.at[j, t], down).wait_recv()

    for t in range(2):
        loads[t].wait()
        trades[t].wait_recv()

        @pl.when(has_up)
        def _():
            kv_z(0, t).start()

        @pl.when(even)
        def _():
            kv_y(0, t, 0).start()

    row_pos = chip * rows + lax.broadcasted_iota(jnp.int32, (rows, rows), 0)

    def next_doc(i, carry):
        end, start = carry
        end = end + len_ref[i]
        return end, jnp.where(row_pos >= end, end, start)

    _, doc_start = lax.fori_loop(
        0, len_ref.shape[0], next_doc,
        (jnp.int32(0), jnp.zeros((rows, rows), jnp.int32)))
    for j in range(SLOTS):
        key_pos = (chip - j) * rows + lax.broadcasted_iota(jnp.int32, (rows, rows), 1)
        allowed = key_pos >= doc_start
        if j == 0:
            allowed = allowed & (key_pos <= row_pos)
        bias[j] = jnp.where(allowed, 0.0, MASKED_SCORE)

    for j in range(1, SLOTS):
        @pl.when(chip < j)
        def _():
            k_buf[slot(j)] = jnp.zeros((rows, HEAD_DIM), BF16)
            v_buf[slot(j)] = jnp.zeros((rows, HEAD_DIM), BF16)

    for i in range(2, 4):
        loads[i].wait()
        trades[i].wait_recv()

    def block(j):
        for h in range(PER_GROUP):
            hr = slice(h * rows, (h + 1) * rows)
            hc = slice(h * HEAD_DIM, (h + 1) * HEAD_DIM)
            jc = slice(j * rows, (j + 1) * rows)
            s = dot_nt(q_buf[:, hc], k_buf[jc]) * SCALE + bias[j]
            m = jnp.max(s, axis=1, keepdims=True)
            e = jnp.exp(s - m)
            e_scr[hr, jc] = e
            m_scr[j, h] = m
            l_scr[j, h] = jnp.sum(e, axis=1, keepdims=True)
            dp_scr[hr, jc] = dot_nt(g_buf[:, hc], v_buf[jc])

    block(0)
    for h in range(PER_GROUP):
        hr = slice(h * rows, (h + 1) * rows)
        hc = slice(h * HEAD_DIM, (h + 1) * HEAD_DIM)
        qt[:, hr] = q_buf[:, hc].astype(F32).T.astype(BF16)
        gt[:, hr] = g_buf[:, hc].astype(F32).T.astype(BF16)

    @pl.when(has_down)
    def _():
        for t in range(2):
            kv_arrived(2, t)

            @pl.when(has_up)
            def _():
                kv_z(1, t).start()

            @pl.when(even)
            def _():
                kv_y(1, t, 2).start()

            @pl.when(odd)
            def _():
                kv_y(0, t, 2).start()

    block(2)

    @pl.when(chip >= 1)
    def _():
        for t in range(2):
            kv_arrived(1, t)

    block(1)

    @pl.when(chip >= 4)
    def _():
        for t in range(2):
            kv_arrived(4, t)

            @pl.when(odd)
            def _():
                kv_y(1, t, 4).start()

    block(4)

    @pl.when(chip >= 3)
    def _():
        for t in range(2):
            kv_arrived(3, t)

    block(3)

    for h in range(PER_GROUP):
        m = m_scr[0, h]
        for j in range(1, SLOTS):
            m = jnp.maximum(m, m_scr[j, h])
        scaled = [jnp.exp(m_scr[j, h] - m) for j in range(SLOTS)]
        total = scaled[0] * l_scr[0, h]
        for j in range(1, SLOTS):
            total = total + scaled[j] * l_scr[j, h]
        inverse = 1.0 / total
        for j in range(SLOTS):
            f_scr[j, h] = scaled[j] * inverse

    def grad_y(msg, t):
        return remote(part.at[3 - 2 * msg, t], y_got.at[msg, t],
                      gy_send.at[msg, t], gy_recv.at[msg, t], side)

    def grad_z(msg, t):
        return remote(part.at[4 - 2 * msg, t], z_got.at[msg, t],
                      gz_send.at[msg, t], gz_recv.at[msg, t], down)

    def value_term(j):
        jc = slice(j * rows, (j + 1) * rows)
        for h in range(PER_GROUP):
            hr = slice(h * rows, (h + 1) * rows)
            w = e_scr[hr, jc] * f_scr[j, h]
            e_scr[hr, jc] = w
            w_scr[hr, jc] = w.astype(BF16)
        part[j, 0] = dot_nn(gt[...], w_scr[:, jc])

    def key_term(j, deltas):
        jc = slice(j * rows, (j + 1) * rows)
        for h in range(PER_GROUP):
            hr = slice(h * rows, (h + 1) * rows)
            ds_scr[hr, jc] = (e_scr[hr, jc] * (dp_scr[hr, jc] - deltas[h])).astype(BF16)
        part[j, 1] = dot_nn(qt[...], ds_scr[:, jc])

    def send_y(msg, t):
        @pl.when(chip >= 3 - 2 * msg)
        def _():
            grad_y(msg, t).start()

    def relay_far(t):
        @pl.when(chip >= 4)
        def _():
            @pl.when(odd)
            def _():
                grad_y(0, t).wait_recv()
                part[4, t] += y_got[0, t]

            grad_z(0, t).start()

    def relay_near(t):
        @pl.when(has_down)
        def _():
            @pl.when(even)
            def _():
                grad_y(0, t).wait_recv()
                part[2, t] += y_got[0, t]

            @pl.when(odd)
            def _():
                grad_y(1, t).wait_recv()
                part[2, t] += y_got[1, t]

            @pl.when(has_up)
            def _():
                grad_z(0, t).wait_recv()
                part[2, t] += z_got[0, t]

            grad_z(1, t).start()

    def finish(t):
        @pl.when(even)
        def _():
            grad_y(1, t).wait_recv()
            part[0, t] += y_got[1, t]

        @pl.when(has_up)
        def _():
            grad_z(1, t).wait_recv()
            part[0, t] += z_got[1, t]

    outs = ((att_s, att_out, width), (dq_s, dq_out, width), (dv_s, dv_out, HEAD_DIM), (dk_s, dk_out, HEAD_DIM))

    def out_copies(i):
        src, dst, size = outs[i]
        return (
            pltpu.make_async_copy(src.at[own_rows(core), :], dst.at[:, cols(core, size)], out_local.at[i]),
            remote(src.at[own_rows(1 - core), :], dst.at[:, cols(core, size)],
                   out_send.at[i], out_recv.at[i], sib),
        )

    value_term(3)
    send_y(0, 0)
    value_term(4)

    @pl.when(even)
    def _():
        relay_far(0)

    value_term(1)
    send_y(1, 0)
    value_term(2)
    value_term(0)

    deltas = []
    for h in range(PER_GROUP):
        hr = slice(h * rows, (h + 1) * rows)
        hc = slice(h * HEAD_DIM, (h + 1) * HEAD_DIM)
        o = dot_nn(w_scr[hr], v_buf[...]).astype(BF16)
        att_s[:, hc] = o
        deltas.append(jnp.sum(o.astype(F32) * g_buf[:, hc].astype(F32), axis=1, keepdims=True))
    for copy in out_copies(0):
        copy.start()

    key_term(3, deltas)
    send_y(0, 1)
    key_term(4, deltas)

    @pl.when(even)
    def _():
        relay_far(1)

    key_term(1, deltas)
    send_y(1, 1)

    @pl.when(odd)
    def _():
        relay_far(0)

    key_term(2, deltas)
    key_term(0, deltas)
    for h in range(PER_GROUP):
        hr = slice(h * rows, (h + 1) * rows)
        hc = slice(h * HEAD_DIM, (h + 1) * HEAD_DIM)
        dq_s[:, hc] = (dot_nn(ds_scr[hr], k_buf[...]) * SCALE).astype(BF16)
    for copy in out_copies(1):
        copy.start()

    @pl.when(odd)
    def _():
        relay_far(1)

    relay_near(0)
    relay_near(1)
    finish(0)
    dv_s[...] = part[0, 0].T.astype(BF16)
    for copy in out_copies(2):
        copy.start()
    finish(1)
    dk_s[...] = (part[0, 1].T * SCALE).astype(BF16)
    for copy in out_copies(3):
        copy.start()

    for trade in trades:
        trade.wait_send()
    for t in range(2):
        @pl.when(has_up)
        def _():
            kv_z(0, t).wait_send()

        @pl.when(has_up & has_down)
        def _():
            kv_z(1, t).wait_send()

        @pl.when(even | has_down)
        def _():
            kv_y(0, t, 0).wait_send()

        @pl.when((even & has_down) | (odd & (chip >= 4)))
        def _():
            kv_y(1, t, 2).wait_send()

        for msg in range(2):
            @pl.when(chip >= 3 - 2 * msg)
            def _():
                grad_y(msg, t).wait_send()

            @pl.when(chip >= 4 - 2 * msg)
            def _():
                grad_z(msg, t).wait_send()
    for i in range(4):
        local, sent = out_copies(i)
        local.wait()
        sent.wait()


def solution(mesh):
    chips = mesh.shape["ctx"] // 2

    def on_device(queries, keys, values, lengths, d_out):
        tok = queries.shape[0]
        rows = 2 * tok
        width = PER_GROUP * HEAD_DIM
        stacked = PER_GROUP * rows
        window = SLOTS * rows
        dma = pltpu.SemaphoreType.DMA
        vmem = pltpu.VMEM
        anywhere = pl.BlockSpec(memory_space=pl.ANY)
        attended, grad_q, grad_k, grad_v = pl.pallas_call(
            functools.partial(kernel, chips),
            out_shape=(
                jax.ShapeDtypeStruct(queries.shape, BF16),
                jax.ShapeDtypeStruct(queries.shape, BF16),
                jax.ShapeDtypeStruct(keys.shape, BF16),
                jax.ShapeDtypeStruct(keys.shape, BF16),
            ),
            in_specs=[pl.BlockSpec(memory_space=pltpu.SMEM)] + [anywhere] * 4,
            out_specs=(anywhere,) * 4,
            scratch_shapes=[
                vmem((window, HEAD_DIM), BF16),
                vmem((window, HEAD_DIM), BF16),
                vmem((rows, width), BF16),
                vmem((rows, width), BF16),
                vmem((HEAD_DIM, stacked), BF16),
                vmem((HEAD_DIM, stacked), BF16),
                vmem((SLOTS, rows, rows), F32),
                vmem((stacked, window), F32),
                vmem((stacked, window), F32),
                vmem((stacked, window), BF16),
                vmem((stacked, window), BF16),
                vmem((SLOTS, PER_GROUP, rows, 1), F32),
                vmem((SLOTS, PER_GROUP, rows, 1), F32),
                vmem((SLOTS, PER_GROUP, rows, 1), F32),
                vmem((SLOTS, 2, HEAD_DIM, rows), F32),
                vmem((2, 2, HEAD_DIM, rows), F32),
                vmem((2, 2, HEAD_DIM, rows), F32),
                vmem((rows, width), BF16),
                vmem((rows, width), BF16),
                vmem((rows, HEAD_DIM), BF16),
                vmem((rows, HEAD_DIM), BF16),
                dma((4,)), dma((4,)), dma((4,)),
                dma((SLOTS, 2)), dma((2, 2)), dma((2, 2)),
                dma((2, 2)), dma((2, 2)), dma((2, 2)), dma((2, 2)),
                dma((4,)), dma((4,)), dma((4,)),
            ],
            compiler_params=pltpu.CompilerParams(
                collective_id=0, has_side_effects=True, vmem_limit_bytes=48 * 2**20
            ),
        )(lengths, queries, keys, values, d_out)
        return attended, grad_q, grad_k, grad_v

    rows_split = P(("groups", "ctx"), None)
    return jax.shard_map(
        on_device, mesh=mesh,
        in_specs=(rows_split, rows_split, rows_split, P("groups"), rows_split),
        out_specs=(rows_split,) * 4, check_vma=False,
    )
```
